32 devices in a mesh: ctx: 8 (over z, x), ch: 4 (over y, core).
Axes of the slice: x: 2, y: 2, z: 4, core: 2. Of those that a mesh axis runs over, the one named last changes fastest.
Arguments:
- tokens: bfloat16 [1024, 4096], P('ctx'), may hold values from -6 to 6
- projections: bfloat16 [3, 4096, 4096], P(None, 'ctx', 'ch'), may hold values from -0.09375 to 0.09375
- decay_rates: float32 [4096, 16], P('ch'), may hold values from 0.00048828125 to 0.03
- residues: float32 [4096, 16], P('ch'), may hold values from -1.5 to 1.5
- short_filter: bfloat16 [4096, 128], P('ch'), may hold values from -0.5 to 0.5
Outputs:
- mixed: bfloat16 [1024, 4096], P('ctx', 'ch')
The draws below stay inside these ranges and needn't reach their ends.
All inputs are finite; a program needn't handle non-finite values.
Results may differ from the reference program's by a relative error of at most 0.0068.
Values may be sent and summed in bfloat16 or wider, within the bound.
A program may use at most 64 MiB of HBM per device.

```python
import math
import jax
import jax.numpy as jnp
from jax import lax

D = 4096
MODES = 16
MR = 128
TOKENS = 1024


def level_of(stream_key, dims, split, least, top_value):
    factor_of = 1.0
    for axis_at, shards_of in split:
        steps = jax.random.uniform(jax.random.fold_in(jax.random.fold_in(stream_key, 6), axis_at), (shards_of,), jnp.float32, least / len(split), top_value / len(split))
        factor_of = factor_of * jnp.repeat(jnp.exp(steps), dims[axis_at] // shards_of).reshape((-1,) + (1,) * (len(dims) - 1 - axis_at))
    return factor_of


def centred(key, extent, deviation, most, cuts=(), held_as=jnp.bfloat16):
    result = jax.random.normal(key, extent, jnp.float32) * deviation
    if len(cuts) > 0:
        result = level_of(key, extent, cuts, -0.22, 0.18) * result
    return jnp.clip(result, min=-most, max=most).astype(held_as)


def setup_inputs(seed: int = 0) -> dict:
    key_list = jax.random.split(jax.random.key(seed), 6)
    tokens = centred(key_list[0], (TOKENS, D), 1.0, 6.0, ((0, 8),))
    projections = centred(key_list[1], (3, D, D), D ** -0.5, 0.09375, ((1, 8), (2, 4)))
    decay_rates = jnp.clip(jnp.exp(math.log(0.03) - 4.118061 * jax.random.uniform(key_list[2], (D, MODES), jnp.float32) ** level_of(key_list[2], (D, MODES), ((0, 4),), -0.2, 0.2)), 0.00048828125, 0.03)
    residues = centred(key_list[3], (D, MODES), 0.25, 1.5, ((0, 4),), jnp.float32)
    short_filter = centred(key_list[4], (D, MR), MR ** -0.5, 0.5, ((0, 4),))
    return dict(tokens=tokens, projections=projections, decay_rates=decay_rates, residues=residues, short_filter=short_filter)


def impulse_rows(rate_rows, residue_rows):
    positions = jnp.arange(TOKENS, dtype=jnp.float32)[None, :]

    def add_mode(mode_index, running):
        mode_rate = lax.dynamic_slice_in_dim(rate_rows, mode_index, 1, 1)
        weight = lax.dynamic_slice_in_dim(residue_rows, mode_index, 1, 1)
        return running + weight * jnp.sqrt(2.0 * mode_rate) * jnp.exp(-mode_rate * positions)
    start_value = jnp.zeros((rate_rows.shape[0], TOKENS), jnp.float32)
    return lax.fori_loop(0, MODES, add_mode, start_value)

def long_convolution(operands):
    signal, rate_rows, residue_rows = operands
    impulse = impulse_rows(rate_rows, residue_rows)
    spectrum = jnp.fft.rfft(signal, n=2 * TOKENS, axis=1) * jnp.fft.rfft(impulse, n=2 * TOKENS, axis=1)
    return jnp.fft.irfft(spectrum, n=2 * TOKENS, axis=1)[:, :TOKENS]

def reference(tokens, projections, decay_rates, residues, short_filter):
    gate_in = jnp.dot(tokens, projections[0], preferred_element_type=jnp.float32).astype(jnp.bfloat16)
    values = jnp.dot(tokens, projections[1], preferred_element_type=jnp.float32).astype(jnp.bfloat16)
    gate_out = jnp.dot(tokens, projections[2], preferred_element_type=jnp.float32).astype(jnp.bfloat16)
    signal = (gate_in.astype(jnp.float32) * values.astype(jnp.float32)).T
    block_width = min(D, 256)
    groups = D // block_width
    convolved = lax.map(long_convolution, (signal.reshape(groups, block_width, TOKENS), decay_rates.reshape(groups, block_width, MODES), residues.reshape(groups, block_width, MODES)))
    convolved = convolved.reshape(D, TOKENS).T
    gated_rows = (gate_out.astype(jnp.float32) * convolved).astype(jnp.bfloat16)
    padded = jnp.pad(gated_rows.astype(jnp.float32), ((MR - 1, 0), (0, 0)))
    tap_table = short_filter.astype(jnp.float32)

    def add_tap(tap_index, running):
        offset = MR - 1 - tap_index
        shifted = lax.dynamic_slice_in_dim(padded, offset, TOKENS, 0)
        weight = lax.dynamic_slice_in_dim(tap_table, tap_index, 1, 1)[:, 0]
        return running + shifted * weight[None, :]
    filtered = lax.fori_loop(0, MR, add_tap, jnp.zeros((TOKENS, D), jnp.float32))
    return filtered.astype(jnp.bfloat16)
```

```python
import functools
import math

import jax
import jax.numpy as jnp
from jax import lax
from jax.experimental import pallas as pl
from jax.experimental.pallas import tpu as pltpu
from jax.sharding import PartitionSpec as P

MESH = pl.DeviceIdType.MESH
PAIR = 2
CHUNKS = 8
LANES = 128


def remote(src, dst, send_sem, recv_sem, device):
    return pltpu.make_async_remote_copy(
        src_ref=src, dst_ref=dst, send_sem=send_sem, recv_sem=recv_sem,
        device_id=device, device_id_type=MESH,
    )


def project_kernel(
    tok_ref, proj_ref, signal_ref, gate_ref,
    tokb, wbuf, part, sendb, recvb,
    local_sem, wl_sem, ws_sem, wr_sem,
    tzs, tzr, txs, txr, tcs, tcr, ps_sem, pr_sem,
):
    rows = tok_ref.shape[0]
    depth = proj_ref.shape[1]
    width = wbuf.shape[3]
    span = PAIR * depth
    ctx_count = lax.axis_size("ctx")
    zc = ctx_count // PAIR
    seq = rows * ctx_count
    ctx = lax.axis_index("ctx")
    ch = lax.axis_index("ch")
    mz, mx = ctx // PAIR, ctx % PAIR
    core = ch % 2
    mate = {"ch": ch + 1 - 2 * core}
    across = {"ctx": ctx + 1 - 2 * mx}
    half = rows // 2
    low = (mz < zc // 2).astype(jnp.int32)

    def at_z(z):
        return {"ctx": z * PAIR + mx}

    def order(i):
        return low * (zc - 1 - i) + (1 - low) * i

    def cols(z):
        return pl.ds(pl.multiple_of(z * span, 128), span)

    def block(z, x):
        return pl.ds(pl.multiple_of((z * PAIR + x) * rows, 16), rows)

    def half_block(z, x):
        return pl.ds(pl.multiple_of((z * PAIR + x) * rows + core * half, 16), half)

    def group(d, x):
        return pl.ds(pl.multiple_of((d * PAIR + x) * width, 128), width)

    k_rows = pl.ds(pl.multiple_of(mx * depth, 16), depth)
    my_half = pl.ds(pl.multiple_of(core * half, 16), half)

    own_tok = pltpu.make_async_copy(tok_ref.at[:, cols(mz)], tokb.at[block(mz, mx)], local_sem)
    own_tok.start()
    own_w = []
    for i in range(zc):
        d = order(i)
        own_w.append(
            pltpu.make_async_copy(
                proj_ref.at[:, :, group(d, mx)], wbuf.at[d, :, k_rows], wl_sem.at[i]
            )
        )
        own_w[-1].start()

    barrier = pltpu.get_barrier_semaphore()
    for o in range(1, zc):
        pl.semaphore_signal(
            barrier, inc=1, device_id=at_z((mz + o) % zc), device_id_type=MESH
        )
    pl.semaphore_signal(barrier, inc=1, device_id=across, device_id_type=MESH)
    pl.semaphore_signal(barrier, inc=1, device_id=mate, device_id_type=MESH)
    pl.semaphore_wait(barrier, zc + 1)

    sent = []
    z_copy, x_copy, c_copy, w_copy = {}, {}, {}, {}
    for o in range(1, zc):
        zt = (mz + o) % zc
        z_copy[o] = remote(
            tok_ref.at[my_half, cols(zt)], tokb.at[half_block(mz, mx)],
            tzs.at[o], tzr.at[o], at_z(zt),
        )
        z_copy[o].start()
    x_copy[0] = remote(
        tok_ref.at[my_half, cols(mz)], tokb.at[half_block(mz, mx)],
        txs.at[0], txr.at[0], across,
    )
    x_copy[0].start()

    def send_weights(i):
        d = order(i)
        w_copy[i] = remote(
            proj_ref.at[:, :, group(d, 1 - mx)], wbuf.at[d, :, k_rows],
            ws_sem.at[i], wr_sem.at[i], across,
        )
        w_copy[i].start()

    send_weights(0)
    for o in range(1, zc):
        zs = (mz + zc - o) % zc
        z_copy[o].wait_recv()
        here = tokb.at[half_block(zs, mx)]
        x_copy[o] = remote(here, here, txs.at[o], txr.at[o], across)
        x_copy[o].start()
        c_copy[o] = remote(here, here, tcs.at[o], tcr.at[o], mate)
        c_copy[o].start()
    for i in range(1, zc):
        send_weights(i)
    for o in range(zc):
        zs = (mz + zc - o) % zc
        x_copy[o].wait_recv()
        here = tokb.at[half_block(zs, 1 - mx)]
        c_copy[zc + o] = remote(here, here, tcs.at[zc + o], tcr.at[zc + o], mate)
        c_copy[zc + o].start()
    for key in c_copy:
        c_copy[key].wait_recv()
    own_tok.wait()

    tile = math.gcd(seq, 256)
    interior = jnp.logical_and(mz > 0, mz < zc - 1)
    at_end = jnp.logical_or(mz == 0, mz == zc - 1)

    def hop(d):
        right = (d > mz).astype(jnp.int32)
        to = mz + 2 * right - 1
        last = (d == to).astype(jnp.int32) * (1 - right)
        slot = d + last * (zc - d)
        return remote(sendb.at[d], recvb.at[slot], ps_sem.at[d], pr_sem.at[slot], at_z(to))

    def incoming(slot):
        return remote(sendb.at[0], recvb.at[slot], ps_sem.at[0], pr_sem.at[slot], at_z(mz))

    def tile_rows(t):
        return pl.ds(pl.multiple_of(t * tile, 16), tile)

    for i in range(zc):
        d = order(i)
        own_w[i].wait()
        w_copy[i].wait_recv()

        @pl.loop(0, seq // tile)
        def _(t):
            here = tile_rows(t)
            block_tok = tokb[here, :]
            for k in range(3):
                part[d, k, here, :] = jnp.dot(
                    block_tok, wbuf[d, k], preferred_element_type=jnp.float32
                )

        @pl.when(jnp.logical_and(at_end, d != mz))
        def _():
            @pl.loop(0, seq // tile)
            def _(t):
                here = tile_rows(t)
                for k in range(3):
                    sendb[d, k, here, :] = part[d, k, here, :].astype(jnp.bfloat16)

            hop(d).start()

    def forward(d, wanted):
        @pl.when(jnp.logical_and(interior, wanted))
        def _():
            incoming(d).wait_recv()

            @pl.loop(0, seq // tile)
            def _(t):
                here = tile_rows(t)
                for k in range(3):
                    total = part[d, k, here, :] + recvb[d, k, here, :].astype(jnp.float32)
                    sendb[d, k, here, :] = total.astype(jnp.bfloat16)

            hop(d).start()

    for j in range(zc - 1):
        first = low * (zc - 1 - j) + (1 - low) * j
        forward(first, (first - mz) * (2 * low - 1) > 0)
        second = low * j + (1 - low) * (zc - 1 - j)
        forward(second, (second - mz) * (2 * low - 1) < 0)

    def absorb(slot):
        incoming(slot).wait_recv()

        @pl.loop(0, seq // tile)
        def _(t):
            here = tile_rows(t)
            for k in range(3):
                part[mz, k, here, :] += recvb[slot, k, here, :].astype(jnp.float32)

    @pl.when(mz > 0)
    def _():
        absorb(mz)

    @pl.when(mz < zc - 1)
    def _():
        absorb(zc)

    @pl.loop(0, seq // tile)
    def _(t):
        here = tile_rows(t)
        signal_ref[here, :] = part[mz, 0, here, :] * part[mz, 1, here, :]
        gate_ref[here, :] = part[mz, 2, here, :]

    for group_of in (z_copy, x_copy, c_copy, w_copy):
        for key in group_of:
            group_of[key].wait_send()
    for d in range(zc):
        @pl.when(d != mz)
        def _():
            hop(d).wait_send()


def project(tokens, projections):
    rows, features = tokens.shape
    depth, channels = projections.shape[1:]
    ctx_count = lax.axis_size("ctx")
    zc = ctx_count // PAIR
    width = channels // ctx_count
    seq = rows * ctx_count
    dma = pltpu.SemaphoreType.DMA
    shape = jax.ShapeDtypeStruct((seq, width), jnp.float32)
    return pl.pallas_call(
        project_kernel,
        out_shape=(shape, shape),
        in_specs=[pl.BlockSpec(memory_space=pl.ANY)] * 2,
        out_specs=(pl.BlockSpec(memory_space=pltpu.VMEM),) * 2,
        scratch_shapes=[
            pltpu.VMEM((seq, PAIR * depth), jnp.bfloat16),
            pltpu.VMEM((zc, 3, PAIR * depth, width), jnp.bfloat16),
            pltpu.VMEM((zc, 3, seq, width), jnp.float32),
            pltpu.VMEM((zc, 3, seq, width), jnp.bfloat16),
            pltpu.VMEM((zc + 1, 3, seq, width), jnp.bfloat16),
            dma, dma((zc,)), dma((zc,)), dma((zc,)),
            dma((zc,)), dma((zc,)), dma((zc,)), dma((zc,)),
            dma((2 * zc,)), dma((2 * zc,)), dma((zc,)), dma((zc + 1,)),
        ],
        compiler_params=pltpu.CompilerParams(
            collective_id=0, has_side_effects=True, vmem_limit_bytes=48 * 1024 * 1024
        ),
        name="project",
    )(tokens, projections)


def mix_kernel(
    signal_ref, gate_ref, rates_ref, residues_ref, taps_ref, out_ref, gated, taps, mixed
):
    seq, width = signal_ref.shape
    steps = seq // CHUNKS
    modes = rates_ref.shape[1]
    tap_count = taps_ref.shape[1]
    own = pl.ds(pl.multiple_of(lax.axis_index("ctx") * width, 128), width)
    rates = rates_ref[own, :].T
    weights = residues_ref[own, :].T * jnp.sqrt(2.0 * rates)
    taps[...] = taps_ref[own, :].astype(jnp.float32).T
    wide = (CHUNKS, width)
    decay = jnp.exp(-rates)
    decays = [jnp.broadcast_to(decay[m : m + 1], wide) for m in range(modes)]
    gains = [jnp.broadcast_to(weights[m : m + 1], wide) for m in range(modes)]
    ids = lax.broadcasted_iota(jnp.int32, wide, 0)

    def row(ref, s):
        return ref[pl.ds(s, CHUNKS, stride=steps), :]

    def advance(s, states):
        x = row(signal_ref, s)
        return tuple(decays[m] * states[m] + x for m in range(modes))

    zero = jnp.zeros(wide, jnp.float32)
    ends = lax.fori_loop(0, steps, advance, (zero,) * modes, unroll=4)
    starts = []
    for m in range(modes):
        total = ends[m]
        shift = 1
        while shift < CHUNKS:
            factor = jnp.exp(-rates[m : m + 1] * float(steps * shift))
            total = total + jnp.where(ids >= shift, factor * pltpu.roll(total, shift, 0), 0.0)
            shift *= 2
        starts.append(jnp.where(ids >= 1, pltpu.roll(total, 1, 0), 0.0))

    def emit(s, states):
        states = advance(s, states)
        terms = [gains[m] * states[m] for m in range(modes)]
        while len(terms) > 1:
            terms = [a + b for a, b in zip(terms[::2], terms[1::2])] + terms[len(terms) & ~1 :]
        value = (row(gate_ref, s) * terms[0]).astype(jnp.bfloat16).astype(jnp.float32)
        gated[steps + s] = value
        gated[s] = jnp.where(ids >= 1, pltpu.roll(value, 1, 0), 0.0)
        return states

    lax.fori_loop(0, steps, emit, tuple(starts), unroll=2)

    out_block, tap_block = 16, 8

    @pl.loop(0, steps // out_block)
    def _(b):
        base = b * out_block

        def add_taps(kb, sums):
            first = steps + base - kb * tap_block - (tap_block - 1)
            window = [gated[first + i] for i in range(out_block + tap_block - 1)]
            sums = list(sums)
            for k in range(tap_block):
                tap = jnp.broadcast_to(taps[pl.ds(kb * tap_block + k, 1), :], wide)
                for i in range(out_block):
                    sums[i] = sums[i] + tap * window[i + tap_block - 1 - k]
            return tuple(sums)

        sums = lax.fori_loop(0, tap_count // tap_block, add_taps, (zero,) * out_block)
        for i in range(out_block):
            mixed[pl.ds(base + i, CHUNKS, stride=steps), :] = sums[i]

    out_ref[...] = mixed[...].astype(out_ref.dtype)


def mix(signal, gate, decay_rates, residues, short_filter):
    seq, width = signal.shape
    steps = seq // CHUNKS
    tap_count = short_filter.shape[1]
    return pl.pallas_call(
        mix_kernel,
        out_shape=jax.ShapeDtypeStruct((seq, width), jnp.bfloat16),
        in_specs=[pl.BlockSpec(memory_space=pltpu.VMEM)] * 5,
        out_specs=pl.BlockSpec(memory_space=pltpu.VMEM),
        scratch_shapes=[
            pltpu.VMEM((2 * steps, CHUNKS, width), jnp.float32),
            pltpu.VMEM((tap_count, width), jnp.float32),
            pltpu.VMEM((seq, width), jnp.float32),
        ],
        compiler_params=pltpu.CompilerParams(vmem_limit_bytes=32 * 1024 * 1024),
        name="mix",
    )(signal, gate, decay_rates, residues, short_filter)


def spread_kernel(mixed_ref, out_ref, local_sem, send_sem, recv_sem):
    ctx_count = lax.axis_size("ctx")
    ctx = lax.axis_index("ctx")
    rows = out_ref.shape[0]
    width = mixed_ref.shape[1]
    mine = pl.ds(pl.multiple_of(ctx * width, 128), width)

    def rows_of(p):
        return pl.ds(pl.multiple_of(p * rows, 16), rows)

    own = pltpu.make_async_copy(mixed_ref.at[rows_of(ctx)], out_ref.at[:, mine], local_sem)
    own.start()
    barrier = pltpu.get_barrier_semaphore()
    peers = [(ctx + o) % ctx_count for o in range(1, ctx_count)]
    for p in peers:
        pl.semaphore_signal(barrier, inc=1, device_id={"ctx": p}, device_id_type=MESH)
    pl.semaphore_wait(barrier, ctx_count - 1)
    copies = []
    for o, p in enumerate(peers):
        copies.append(
            remote(
                mixed_ref.at[rows_of(p)], out_ref.at[:, mine],
                send_sem.at[o], recv_sem.at[o], {"ctx": p},
            )
        )
        copies[-1].start()
    own.wait()
    for copy in copies:
        copy.wait()


def spread(mixed, channels):
    seq, width = mixed.shape
    ctx_count = lax.axis_size("ctx")
    dma = pltpu.SemaphoreType.DMA
    return pl.pallas_call(
        spread_kernel,
        out_shape=jax.ShapeDtypeStruct((seq // ctx_count, channels), mixed.dtype),
        in_specs=[pl.BlockSpec(memory_space=pltpu.VMEM)],
        out_specs=pl.BlockSpec(memory_space=pltpu.VMEM),
        scratch_shapes=[dma, dma((ctx_count - 1,)), dma((ctx_count - 1,))],
        compiler_params=pltpu.CompilerParams(collective_id=1, has_side_effects=True),
        name="spread",
    )(mixed)


def per_device_kernels(tokens, projections, decay_rates, residues, short_filter):
    signal, gate = project(tokens, projections)
    mixed = mix(signal, gate, decay_rates, residues, short_filter)
    return spread(mixed, projections.shape[2])


def kernels_fit(tokens, projections, short_filter):
    ctx_count = lax.axis_size("ctx")
    ch_count = lax.axis_size("ch")
    rows = tokens.shape[0]
    depth, channels = projections.shape[1:]
    steps = rows * ctx_count // CHUNKS
    tap_count = short_filter.shape[1]
    return (
        ctx_count % PAIR == 0 and ctx_count > PAIR and ch_count % 2 == 0
        and channels == ctx_count * LANES and rows % 32 == 0 and depth % 128 == 0
        and steps % 16 == 0 and tap_count % 8 == 0 and tap_count <= steps
        and rows * ctx_count <= 2048
    )


two_pi = 2.0 * math.pi
highest = lax.Precision.HIGHEST


def angle_table(first_ids, second_ids, length):
    products = first_ids[:, None] * second_ids[None, :] % length
    angles = products.astype(jnp.float32) * (two_pi / length)
    return (jnp.cos(angles), jnp.sin(angles))


def twist(real_part, imag_part, cosine_table, sine_table, direction):
    return (
        real_part * cosine_table - direction * imag_part * sine_table,
        imag_part * cosine_table + direction * real_part * sine_table,
    )


def complex_apply(einsum_form, cosine_table, sine_table, real_part, imag_part, direction):
    cos_real = jnp.einsum(einsum_form, cosine_table, real_part, precision=highest)
    cos_imag = jnp.einsum(einsum_form, cosine_table, imag_part, precision=highest)
    sin_real = jnp.einsum(einsum_form, sine_table, real_part, precision=highest)
    sin_imag = jnp.einsum(einsum_form, sine_table, imag_part, precision=highest)
    return (cos_real - direction * sin_imag, cos_imag + direction * sin_real)


def filter_values(positions, rates_t, residues_t):
    terms = residues_t * jnp.sqrt(2.0 * rates_t) * jnp.exp(-rates_t * positions[None])
    return jnp.sum(terms, axis=0)


def toeplitz(taps_table):
    channels = taps_table.shape[0]
    tap_count = taps_table.shape[1]
    zero_block = jnp.zeros((channels, tap_count), taps_table.dtype)
    unrolled = jnp.concatenate([zero_block, jnp.flip(taps_table, axis=1), zero_block], axis=1)
    tiled = jnp.tile(unrolled, (1, tap_count))
    tiled = tiled[:, : tap_count * (3 * tap_count - 1)].reshape(
        channels, tap_count, 3 * tap_count - 1
    )
    return tiled[:, :, tap_count - 1 : 3 * tap_count - 1]


def project_general(tokens, projections):
    einsum_form = "td,kdc->kct"
    running = jnp.einsum(
        einsum_form,
        tokens,
        lax.all_gather(projections, "ctx", axis=1, tiled=True),
        preferred_element_type=jnp.float32,
    )
    return running.astype(jnp.bfloat16)


def per_device_general(tokens, projections, decay_rates, residues, short_filter):
    ctx_count = lax.axis_size("ctx")
    ctx_index = lax.axis_index("ctx")
    tok_rows = tokens.shape[0]
    channels = projections.shape[2]
    group_width = channels // ctx_count
    block_count = 2 * ctx_count
    full_length = tok_rows * block_count
    seq_length = tok_rows * ctx_count
    tap_count = short_filter.shape[1]
    block_ids = jnp.arange(block_count, dtype=jnp.int32)
    source_ids = jnp.arange(ctx_count, dtype=jnp.int32)
    row_ids = jnp.arange(tok_rows, dtype=jnp.int32)
    cos_block, sin_block = angle_table(block_ids, source_ids, block_count)
    cos_row, sin_row = angle_table(row_ids, row_ids, tok_rows)
    streams = project_general(tokens, projections)
    arrived_streams = lax.all_to_all(streams, "ctx", split_axis=1, concat_axis=2, tiled=True)
    signal = arrived_streams[0].astype(jnp.float32) * arrived_streams[1].astype(jnp.float32)
    own_rates = lax.dynamic_slice_in_dim(decay_rates, ctx_index * group_width, group_width, 0)
    own_residues = lax.dynamic_slice_in_dim(residues, ctx_index * group_width, group_width, 0)
    positions = jnp.arange(seq_length, dtype=jnp.float32)[None, :]
    impulse = filter_values(positions, own_rates.T[:, :, None], own_residues.T[:, :, None])
    cos_twist, sin_twist = angle_table(block_ids, row_ids, full_length)

    def to_spectrum(sequence_values):
        shaped = sequence_values.reshape(group_width, ctx_count, tok_rows)
        real_part = jnp.einsum("aq,cqr->car", cos_block, shaped, precision=highest)
        imag_part = -jnp.einsum("aq,cqr->car", sin_block, shaped, precision=highest)
        real_part, imag_part = twist(real_part, imag_part, cos_twist, sin_twist, -1.0)
        return complex_apply("br,car->cab", cos_row, sin_row, real_part, imag_part, -1.0)

    signal_real, signal_imag = to_spectrum(signal)
    impulse_real, impulse_imag = to_spectrum(impulse)
    product_real = signal_real * impulse_real - signal_imag * impulse_imag
    product_imag = signal_real * impulse_imag + signal_imag * impulse_real
    back_real, back_imag = complex_apply(
        "br,cab->car", cos_row, sin_row, product_real, product_imag, 1.0
    )
    back_real, back_imag = twist(back_real, back_imag, cos_twist, sin_twist, 1.0)
    convolved = (
        jnp.einsum("aq,car->cqr", cos_block, back_real, precision=highest)
        - jnp.einsum("aq,car->cqr", sin_block, back_imag, precision=highest)
    ) / full_length
    convolved = convolved.reshape(group_width, seq_length)
    gated_rows = (arrived_streams[2].astype(jnp.float32) * convolved).astype(jnp.bfloat16)
    own_taps = lax.dynamic_slice_in_dim(short_filter, ctx_index * group_width, group_width, 0)
    shaped = gated_rows.reshape(group_width, seq_length // tap_count, tap_count)
    previous = jnp.concatenate(
        [jnp.zeros((group_width, 1, tap_count), jnp.bfloat16), shaped[:, :-1]], axis=1
    )
    block_pairs = jnp.concatenate([previous, shaped], axis=2)
    filtered = jnp.einsum(
        "ckj,cbj->bkc", toeplitz(own_taps), block_pairs, preferred_element_type=jnp.float32
    )
    filtered = filtered.reshape(seq_length, group_width).astype(jnp.bfloat16)
    return lax.all_to_all(filtered, "ctx", split_axis=0, concat_axis=1, tiled=True)


def per_device(tokens, projections, decay_rates, residues, short_filter):
    plan = per_device_kernels if kernels_fit(tokens, projections, short_filter) else per_device_general
    return plan(tokens, projections, decay_rates, residues, short_filter)


def solution(mesh):
    in_specs = (P("ctx", None), P(None, "ctx", "ch"), P("ch", None), P("ch", None), P("ch", None))
    out_specs = P("ctx", "ch")
    return jax.shard_map(
        per_device, mesh=mesh, in_specs=in_specs, out_specs=out_specs, check_vma=False
    )
```

```python
import math

import jax
import jax.numpy as jnp
from jax import lax
from jax.experimental import pallas as pl
from jax.experimental.pallas import tpu as pltpu
from jax.sharding import PartitionSpec as P

MESH = pl.DeviceIdType.MESH
PAIR = 2
CHUNKS = 8
LANES = 128
TILE = 256
PIECES = 2


two_pi = 2.0 * math.pi
highest = lax.Precision.HIGHEST


def angle_table(first_ids, second_ids, length):
    products = first_ids[:, None] * second_ids[None, :] % length
    angles = products.astype(jnp.float32) * (two_pi / length)
    return (jnp.cos(angles), jnp.sin(angles))


def twist(real_part, imag_part, cosine_table, sine_table, direction):
    return (
        real_part * cosine_table - direction * imag_part * sine_table,
        imag_part * cosine_table + direction * real_part * sine_table,
    )


def complex_apply(einsum_form, cosine_table, sine_table, real_part, imag_part, direction):
    cos_real = jnp.einsum(einsum_form, cosine_table, real_part, precision=highest)
    cos_imag = jnp.einsum(einsum_form, cosine_table, imag_part, precision=highest)
    sin_real = jnp.einsum(einsum_form, sine_table, real_part, precision=highest)
    sin_imag = jnp.einsum(einsum_form, sine_table, imag_part, precision=highest)
    return (cos_real - direction * sin_imag, cos_imag + direction * sin_real)


def filter_values(positions, rates_t, residues_t):
    terms = residues_t * jnp.sqrt(2.0 * rates_t) * jnp.exp(-rates_t * positions[None])
    return jnp.sum(terms, axis=0)


def toeplitz(taps_table):
    channels = taps_table.shape[0]
    tap_count = taps_table.shape[1]
    zero_block = jnp.zeros((channels, tap_count), taps_table.dtype)
    unrolled = jnp.concatenate([zero_block, jnp.flip(taps_table, axis=1), zero_block], axis=1)
    tiled = jnp.tile(unrolled, (1, tap_count))
    tiled = tiled[:, : tap_count * (3 * tap_count - 1)].reshape(
        channels, tap_count, 3 * tap_count - 1
    )
    return tiled[:, :, tap_count - 1 : 3 * tap_count - 1]


def project_general(tokens, projections):
    einsum_form = "td,kdc->kct"
    running = jnp.einsum(
        einsum_form,
        tokens,
        lax.all_gather(projections, "ctx", axis=1, tiled=True),
        preferred_element_type=jnp.float32,
    )
    return running.astype(jnp.bfloat16)


def per_device_general(tokens, projections, decay_rates, residues, short_filter):
    ctx_count = lax.axis_size("ctx")
    ctx_index = lax.axis_index("ctx")
    tok_rows = tokens.shape[0]
    channels = projections.shape[2]
    group_width = channels // ctx_count
    block_count = 2 * ctx_count
    full_length = tok_rows * block_count
    seq_length = tok_rows * ctx_count
    tap_count = short_filter.shape[1]
    block_ids = jnp.arange(block_count, dtype=jnp.int32)
    source_ids = jnp.arange(ctx_count, dtype=jnp.int32)
    row_ids = jnp.arange(tok_rows, dtype=jnp.int32)
    cos_block, sin_block = angle_table(block_ids, source_ids, block_count)
    cos_row, sin_row = angle_table(row_ids, row_ids, tok_rows)
    streams = project_general(tokens, projections)
    arrived_streams = lax.all_to_all(streams, "ctx", split_axis=1, concat_axis=2, tiled=True)
    signal = arrived_streams[0].astype(jnp.float32) * arrived_streams[1].astype(jnp.float32)
    own_rates = lax.dynamic_slice_in_dim(decay_rates, ctx_index * group_width, group_width, 0)
    own_residues = lax.dynamic_slice_in_dim(residues, ctx_index * group_width, group_width, 0)
    positions = jnp.arange(seq_length, dtype=jnp.float32)[None, :]
    impulse = filter_values(positions, own_rates.T[:, :, None], own_residues.T[:, :, None])
    cos_twist, sin_twist = angle_table(block_ids, row_ids, full_length)

    def to_spectrum(sequence_values):
        shaped = sequence_values.reshape(group_width, ctx_count, tok_rows)
        real_part = jnp.einsum("aq,cqr->car", cos_block, shaped, precision=highest)
        imag_part = -jnp.einsum("aq,cqr->car", sin_block, shaped, precision=highest)
        real_part, imag_part = twist(real_part, imag_part, cos_twist, sin_twist, -1.0)
        return complex_apply("br,car->cab", cos_row, sin_row, real_part, imag_part, -1.0)

    signal_real, signal_imag = to_spectrum(signal)
    impulse_real, impulse_imag = to_spectrum(impulse)
    product_real = signal_real * impulse_real - signal_imag * impulse_imag
    product_imag = signal_real * impulse_imag + signal_imag * impulse_real
    back_real, back_imag = complex_apply(
        "br,cab->car", cos_row, sin_row, product_real, product_imag, 1.0
    )
    back_real, back_imag = twist(back_real, back_imag, cos_twist, sin_twist, 1.0)
    convolved = (
        jnp.einsum("aq,car->cqr", cos_block, back_real, precision=highest)
        - jnp.einsum("aq,car->cqr", sin_block, back_imag, precision=highest)
    ) / full_length
    convolved = convolved.reshape(group_width, seq_length)
    gated_rows = (arrived_streams[2].astype(jnp.float32) * convolved).astype(jnp.bfloat16)
    own_taps = lax.dynamic_slice_in_dim(short_filter, ctx_index * group_width, group_width, 0)
    shaped = gated_rows.reshape(group_width, seq_length // tap_count, tap_count)
    previous = jnp.concatenate(
        [jnp.zeros((group_width, 1, tap_count), jnp.bfloat16), shaped[:, :-1]], axis=1
    )
    block_pairs = jnp.concatenate([previous, shaped], axis=2)
    filtered = jnp.einsum(
        "ckj,cbj->bkc", toeplitz(own_taps), block_pairs, preferred_element_type=jnp.float32
    )
    filtered = filtered.reshape(seq_length, group_width).astype(jnp.bfloat16)
    return lax.all_to_all(filtered, "ctx", split_axis=0, concat_axis=1, tiled=True)


def remote(src, dst, send_sem, recv_sem, device):
    return pltpu.make_async_remote_copy(
        src_ref=src, dst_ref=dst, send_sem=send_sem, recv_sem=recv_sem,
        device_id=device, device_id_type=MESH,
    )


def block_kernel(
    tok_ref, proj_ref, rates_ref, residues_ref, filter_ref, out_ref,
    tokb, wbuf, sendb, recvb, ratesb, residuesb, filterb,
    signal, gate, gated, taps, mixed, outb,
    local_sem, par_sem, wl_sem, ws_sem, wr_sem,
    tzs, tzr, txs, txr, tcs, tcr, ps_sem, pr_sem, ol_sem, os_sem, or_sem,
):
    rows = tok_ref.shape[0]
    depth = proj_ref.shape[1]
    width = wbuf.shape[3]
    span = PAIR * depth
    ctx_count = lax.axis_size("ctx")
    zc = ctx_count // PAIR
    held = zc // 2
    seq = rows * ctx_count
    steps = seq // CHUNKS
    tile = sendb.shape[2] // pr_sem.shape[1]
    tiles = seq // tile
    modes = rates_ref.shape[0]
    tap_count = filter_ref.shape[1]
    ctx = lax.axis_index("ctx")
    ch = lax.axis_index("ch")
    mz, mx = ctx // PAIR, ctx % PAIR
    core = ch % 2
    mate = {"ch": ch + 1 - 2 * core}
    across = {"ctx": ctx + 1 - 2 * mx}
    half = rows // 2
    low = (mz < held).astype(jnp.int32)
    at_end = jnp.logical_or(mz == 0, mz == zc - 1)
    interior = jnp.logical_and(mz > 0, mz < zc - 1)

    def at_z(z):
        return {"ctx": z * PAIR + mx}

    def near(j):
        return low * (zc - 1 - j) + (1 - low) * j

    def far(j):
        return low * j + (1 - low) * (zc - 1 - j)

    def order(i):
        return near(i // 2) if i % 2 == 0 else far(i // 2)

    def cols(z):
        return pl.ds(pl.multiple_of(z * span, 128), span)

    def block(z, x):
        return pl.ds(pl.multiple_of((z * PAIR + x) * rows, 16), rows)

    def half_block(z, x):
        return pl.ds(pl.multiple_of((z * PAIR + x) * rows + core * half, 16), half)

    def group(d, x):
        return pl.ds(pl.multiple_of((d * PAIR + x) * width, 128), width)

    def tile_rows(t):
        return pl.ds(pl.multiple_of(t * tile, 16), tile)

    k_rows = pl.ds(pl.multiple_of(mx * depth, 16), depth)
    my_half = pl.ds(pl.multiple_of(core * half, 16), half)

    own_tok = pltpu.make_async_copy(tok_ref.at[:, cols(mz)], tokb.at[block(mz, mx)], local_sem)
    own_tok.start()
    own_w = []
    for i in range(zc):
        d = order(i)
        own_w.append(
            pltpu.make_async_copy(
                proj_ref.at[:, :, group(d, mx)], wbuf.at[d, :, k_rows], wl_sem.at[i]
            )
        )
        own_w[-1].start()
    own_par = []
    for j in range(held):
        place = group(far(j), mx)
        for n, (from_ref, to_ref) in enumerate((
            (rates_ref.at[:, place], ratesb.at[j]),
            (residues_ref.at[:, place], residuesb.at[j]),
            (filter_ref.at[place, :], filterb.at[j]),
        )):
            own_par.append(pltpu.make_async_copy(from_ref, to_ref, par_sem.at[3 * j + n]))
            own_par[-1].start()

    barrier = pltpu.get_barrier_semaphore()
    for o in range(1, ctx_count):
        pl.semaphore_signal(
            barrier, inc=1, device_id={"ctx": (ctx + o) % ctx_count}, device_id_type=MESH
        )
    pl.semaphore_signal(barrier, inc=1, device_id=mate, device_id_type=MESH)
    pl.semaphore_wait(barrier, ctx_count)

    z_copy, x_copy, c_copy, w_copy = {}, {}, {}, {}
    for o in range(1, zc):
        zt = (mz + o) % zc
        z_copy[o] = remote(
            tok_ref.at[my_half, cols(zt)], tokb.at[half_block(mz, mx)],
            tzs.at[o], tzr.at[o], at_z(zt),
        )
        z_copy[o].start()
    x_copy[0] = remote(
        tok_ref.at[my_half, cols(mz)], tokb.at[half_block(mz, mx)],
        txs.at[0], txr.at[0], across,
    )
    x_copy[0].start()

    def send_weights(i):
        d = order(i)
        w_copy[i] = remote(
            proj_ref.at[:, :, group(d, 1 - mx)], wbuf.at[d, :, k_rows],
            ws_sem.at[i], wr_sem.at[i], across,
        )
        w_copy[i].start()

    send_weights(0)
    for o in range(1, zc):
        zs = (mz + zc - o) % zc
        z_copy[o].wait_recv()
        here = tokb.at[half_block(zs, mx)]
        x_copy[o] = remote(here, here, txs.at[o], txr.at[o], across)
        x_copy[o].start()
        c_copy[o] = remote(here, here, tcs.at[o], tcr.at[o], mate)
        c_copy[o].start()
    for i in range(1, zc):
        send_weights(i)
    for o in range(zc):
        zs = (mz + zc - o) % zc
        x_copy[o].wait_recv()
        here = tokb.at[half_block(zs, 1 - mx)]
        c_copy[zc + o] = remote(here, here, tcs.at[zc + o], tcr.at[zc + o], mate)
        c_copy[zc + o].start()
    for key in c_copy:
        c_copy[key].wait_recv()
    own_tok.wait()

    def hop(d, t):
        to = mz + 2 * (d >= held).astype(jnp.int32) - 1
        here = tile_rows(t)
        return remote(
            sendb.at[d, :, here, :], recvb.at[d, :, here, :],
            ps_sem.at[d, t], pr_sem.at[d, t], at_z(to),
        )

    def weights_here(i):
        own_w[i].wait()
        w_copy[i].wait_recv()

    def products(d, t):
        block_tok = tokb[tile_rows(t), :]
        return [
            jnp.dot(block_tok, wbuf[d, k], preferred_element_type=jnp.float32)
            for k in range(3)
        ]

    def arrived(d, t):
        here = tile_rows(t)
        pltpu.make_async_copy(
            sendb.at[d, :, here, :], recvb.at[d, :, here, :], pr_sem.at[d, t]
        ).wait()
        return [recvb[d, k, here, :].astype(jnp.float32) for k in range(3)]

    def pass_on(d, t):
        mine = products(d, t)
        before = arrived(d, t)
        for k in range(3):
            sendb[d, k, tile_rows(t), :] = (mine[k] + before[k]).astype(jnp.bfloat16)
        hop(d, t).start()

    @pl.when(interior)
    def _():
        for j in range(held):
            weights_here(2 * j)
            weights_here(2 * j + 1)

            @pl.loop(0, tiles)
            def _(t):
                pass_on(near(j), t)

                @pl.when(t > 0)
                def _():
                    pass_on(far(j), t - 1)

            pass_on(far(j), tiles - 1)

    wide = (CHUNKS, width)
    zero = jnp.zeros(wide, jnp.float32)
    peers = [(ctx + o) % ctx_count for o in range(1, ctx_count)]
    piece = rows // PIECES

    def leave(j, h, o):
        p = peers[o]
        here = pl.ds(pl.multiple_of(p * rows + h * piece, 16), piece)
        place = far(j) * PAIR + mx
        return remote(
            outb.at[j, here, :], out_ref.at[pl.ds(h * piece, piece), group(far(j), mx)],
            os_sem.at[j, h, o], or_sem.at[place, h], {"ctx": p},
        )

    def stay(j):
        here = pl.ds(pl.multiple_of(ctx * rows, 16), rows)
        return pltpu.make_async_copy(
            outb.at[j, here, :], out_ref.at[:, group(far(j), mx)], ol_sem.at[j]
        )

    def mix(j):
        rates = ratesb[j]
        weights = residuesb[j] * jnp.sqrt(2.0 * rates)
        taps[...] = filterb[j].astype(jnp.float32).T
        decay = jnp.exp(-rates)
        decays = [jnp.broadcast_to(decay[m : m + 1], wide) for m in range(modes)]
        gains = [jnp.broadcast_to(weights[m : m + 1], wide) for m in range(modes)]
        ids = lax.broadcasted_iota(jnp.int32, wide, 0)

        def row(ref, s):
            return ref[pl.ds(s, CHUNKS, stride=steps), :]

        def advance(s, states):
            x = row(signal, s)
            return tuple(decays[m] * states[m] + x for m in range(modes))

        ends = lax.fori_loop(0, steps, advance, (zero,) * modes, unroll=4)
        starts = []
        for m in range(modes):
            total = ends[m]
            shift = 1
            while shift < CHUNKS:
                factor = jnp.exp(-rates[m : m + 1] * float(steps * shift))
                total = total + jnp.where(ids >= shift, factor * pltpu.roll(total, shift, 0), 0.0)
                shift *= 2
            starts.append(jnp.where(ids >= 1, pltpu.roll(total, 1, 0), 0.0))

        def emit(s, states):
            states = advance(s, states)
            terms = [gains[m] * states[m] for m in range(modes)]
            while len(terms) > 1:
                terms = [a + b for a, b in zip(terms[::2], terms[1::2])] + terms[len(terms) & ~1 :]
            value = row(gate, s) * terms[0]
            gated[steps + s] = value
            gated[s] = jnp.where(ids >= 1, pltpu.roll(value, 1, 0), 0.0)
            return states

        lax.fori_loop(0, steps, emit, tuple(starts), unroll=2)

        out_block, tap_block = 16, 8
        for h in range(PIECES):
            @pl.loop(h * piece // out_block, (h + 1) * piece // out_block)
            def _(b):
                base = b * out_block

                def add_taps(kb, sums):
                    first = steps + base - kb * tap_block - (tap_block - 1)
                    window = [gated[first + i] for i in range(out_block + tap_block - 1)]
                    sums = list(sums)
                    for k in range(tap_block):
                        tap = jnp.broadcast_to(taps[pl.ds(kb * tap_block + k, 1), :], wide)
                        for i in range(out_block):
                            sums[i] = sums[i] + tap * window[i + tap_block - 1 - k]
                    return tuple(sums)

                sums = lax.fori_loop(0, tap_count // tap_block, add_taps, (zero,) * out_block)
                for i in range(out_block):
                    mixed[pl.ds(base + i, CHUNKS, stride=steps), :] = sums[i]

            for c in range(CHUNKS):
                here = pl.ds(c * rows + h * piece, piece)
                outb[j, here, :] = mixed[here, :].astype(outb.dtype)
            for o in range(ctx_count - 1):
                leave(j, h, o).start()
        stay(j).start()

    @pl.when(at_end)
    def _():
        for j in range(held):
            weights_here(2 * j)

            @pl.loop(0, tiles)
            def _(t):
                mine = products(near(j), t)
                for k in range(3):
                    sendb[near(j), k, tile_rows(t), :] = mine[k].astype(jnp.bfloat16)
                hop(near(j), t).start()

        for j in range(held):
            weights_here(2 * j + 1)
            for n in range(3):
                own_par[3 * j + n].wait()

            @pl.loop(0, tiles)
            def _(t):
                mine = products(far(j), t)
                before = arrived(far(j), t)
                sums = [mine[k] + before[k] for k in range(3)]
                signal[tile_rows(t), :] = sums[0] * sums[1]
                gate[tile_rows(t), :] = sums[2]

            mix(j)

        for j in range(held):
            stay(j).wait()

            @pl.loop(0, tiles)
            def _(t):
                hop(near(j), t).wait_send()

            for h in range(PIECES):
                for o in range(ctx_count - 1):
                    leave(j, h, o).wait_send()

    @pl.when(interior)
    def _():
        for par in own_par:
            par.wait()
        for j in range(held):
            @pl.loop(0, tiles)
            def _(t):
                hop(near(j), t).wait_send()
                hop(far(j), t).wait_send()

    for group_of in (z_copy, x_copy, c_copy, w_copy):
        for key in group_of:
            group_of[key].wait_send()
    for d in range(zc):
        owner_row = 0 if d < held else zc - 1
        for x in range(PAIR):
            @pl.when(ctx != owner_row * PAIR + x)
            def _():
                for h in range(PIECES):
                    landed = out_ref.at[
                        pl.ds(h * piece, piece), pl.ds((d * PAIR + x) * width, width)
                    ]
                    pltpu.make_async_copy(
                        outb.at[0, pl.ds(0, piece), :], landed, or_sem.at[d * PAIR + x, h]
                    ).wait()


def per_device_kernels(tokens, projections, decay_rates, residues, short_filter):
    rows = tokens.shape[0]
    depth, channels = projections.shape[1:]
    ctx_count = lax.axis_size("ctx")
    zc = ctx_count // PAIR
    held = zc // 2
    width = channels // ctx_count
    seq = rows * ctx_count
    steps = seq // CHUNKS
    tiles = seq // TILE
    modes = decay_rates.shape[1]
    tap_count = short_filter.shape[1]
    dma = pltpu.SemaphoreType.DMA
    f32, bf16 = jnp.float32, jnp.bfloat16
    return pl.pallas_call(
        block_kernel,
        out_shape=jax.ShapeDtypeStruct((rows, channels), bf16),
        in_specs=[pl.BlockSpec(memory_space=pl.ANY)] * 5,
        out_specs=pl.BlockSpec(memory_space=pltpu.VMEM),
        scratch_shapes=[
            pltpu.VMEM((seq, PAIR * depth), bf16),
            pltpu.VMEM((zc, 3, PAIR * depth, width), bf16),
            pltpu.VMEM((zc, 3, seq, width), bf16),
            pltpu.VMEM((zc, 3, seq, width), bf16),
            pltpu.VMEM((held, modes, width), f32),
            pltpu.VMEM((held, modes, width), f32),
            pltpu.VMEM((held, width, tap_count), bf16),
            pltpu.VMEM((seq, width), f32),
            pltpu.VMEM((seq, width), f32),
            pltpu.VMEM((2 * steps, CHUNKS, width), f32),
            pltpu.VMEM((tap_count, width), f32),
            pltpu.VMEM((seq, width), f32),
            pltpu.VMEM((held, seq, width), bf16),
            dma, dma((3 * held,)), dma((zc,)), dma((zc,)), dma((zc,)),
            dma((zc,)), dma((zc,)), dma((zc,)), dma((zc,)),
            dma((2 * zc,)), dma((2 * zc,)), dma((zc, tiles)), dma((zc, tiles)),
            dma((held,)), dma((held, PIECES, ctx_count - 1)), dma((ctx_count, PIECES)),
        ],
        compiler_params=pltpu.CompilerParams(
            collective_id=0, has_side_effects=True, vmem_limit_bytes=48 * 1024 * 1024
        ),
        name="block",
    )(tokens, projections, decay_rates.T, residues.T, short_filter)


def kernels_fit(tokens, projections, short_filter):
    ctx_count = lax.axis_size("ctx")
    rows = tokens.shape[0]
    depth, channels = projections.shape[1:]
    tap_count = short_filter.shape[1]
    return (
        ctx_count == CHUNKS and lax.axis_size("ch") % 2 == 0
        and channels == ctx_count * LANES and rows % (16 * PIECES) == 0 and depth % 128 == 0
        and (rows * ctx_count) % TILE == 0 and tap_count % 8 == 0 and tap_count <= rows
        and rows * ctx_count <= 2048
    )


def per_device(tokens, projections, decay_rates, residues, short_filter):
    plan = per_device_kernels if kernels_fit(tokens, projections, short_filter) else per_device_general
    return plan(tokens, projections, decay_rates, residues, short_filter)


def solution(mesh):
    in_specs = (P("ctx", None), P(None, "ctx", "ch"), P("ch", None), P("ch", None), P("ch", None))
    out_specs = P("ctx", "ch")
    return jax.shard_map(
        per_device, mesh=mesh, in_specs=in_specs, out_specs=out_specs, check_vma=False
    )
```

```python
import math

import jax
import jax.numpy as jnp
from jax import lax
from jax.experimental import pallas as pl
from jax.experimental.pallas import tpu as pltpu
from jax.sharding import PartitionSpec as P

MESH = pl.DeviceIdType.MESH
PAIR = 2
CHUNKS = 8
LANES = 128
TILE = 256
PIECES = 2


two_pi = 2.0 * math.pi
highest = lax.Precision.HIGHEST


def angle_table(first_ids, second_ids, length):
    products = first_ids[:, None] * second_ids[None, :] % length
    angles = products.astype(jnp.float32) * (two_pi / length)
    return (jnp.cos(angles), jnp.sin(angles))


def twist(real_part, imag_part, cosine_table, sine_table, direction):
    return (
        real_part * cosine_table - direction * imag_part * sine_table,
        imag_part * cosine_table + direction * real_part * sine_table,
    )


def complex_apply(einsum_form, cosine_table, sine_table, real_part, imag_part, direction):
    cos_real = jnp.einsum(einsum_form, cosine_table, real_part, precision=highest)
    cos_imag = jnp.einsum(einsum_form, cosine_table, imag_part, precision=highest)
    sin_real = jnp.einsum(einsum_form, sine_table, real_part, precision=highest)
    sin_imag = jnp.einsum(einsum_form, sine_table, imag_part, precision=highest)
    return (cos_real - direction * sin_imag, cos_imag + direction * sin_real)


def filter_values(positions, rates_t, residues_t):
    terms = residues_t * jnp.sqrt(2.0 * rates_t) * jnp.exp(-rates_t * positions[None])
    return jnp.sum(terms, axis=0)


def toeplitz(taps_table):
    channels = taps_table.shape[0]
    tap_count = taps_table.shape[1]
    zero_block = jnp.zeros((channels, tap_count), taps_table.dtype)
    unrolled = jnp.concatenate([zero_block, jnp.flip(taps_table, axis=1), zero_block], axis=1)
    tiled = jnp.tile(unrolled, (1, tap_count))
    tiled = tiled[:, : tap_count * (3 * tap_count - 1)].reshape(
        channels, tap_count, 3 * tap_count - 1
    )
    return tiled[:, :, tap_count - 1 : 3 * tap_count - 1]


def project_general(tokens, projections):
    einsum_form = "td,kdc->kct"
    running = jnp.einsum(
        einsum_form,
        tokens,
        lax.all_gather(projections, "ctx", axis=1, tiled=True),
        preferred_element_type=jnp.float32,
    )
    return running.astype(jnp.bfloat16)


def per_device_general(tokens, projections, decay_rates, residues, short_filter):
    ctx_count = lax.axis_size("ctx")
    ctx_index = lax.axis_index("ctx")
    tok_rows = tokens.shape[0]
    channels = projections.shape[2]
    group_width = channels // ctx_count
    block_count = 2 * ctx_count
    full_length = tok_rows * block_count
    seq_length = tok_rows * ctx_count
    tap_count = short_filter.shape[1]
    block_ids = jnp.arange(block_count, dtype=jnp.int32)
    source_ids = jnp.arange(ctx_count, dtype=jnp.int32)
    row_ids = jnp.arange(tok_rows, dtype=jnp.int32)
    cos_block, sin_block = angle_table(block_ids, source_ids, block_count)
    cos_row, sin_row = angle_table(row_ids, row_ids, tok_rows)
    streams = project_general(tokens, projections)
    arrived_streams = lax.all_to_all(streams, "ctx", split_axis=1, concat_axis=2, tiled=True)
    signal = arrived_streams[0].astype(jnp.float32) * arrived_streams[1].astype(jnp.float32)
    own_rates = lax.dynamic_slice_in_dim(decay_rates, ctx_index * group_width, group_width, 0)
    own_residues = lax.dynamic_slice_in_dim(residues, ctx_index * group_width, group_width, 0)
    positions = jnp.arange(seq_length, dtype=jnp.float32)[None, :]
    impulse = filter_values(positions, own_rates.T[:, :, None], own_residues.T[:, :, None])
    cos_twist, sin_twist = angle_table(block_ids, row_ids, full_length)

    def to_spectrum(sequence_values):
        shaped = sequence_values.reshape(group_width, ctx_count, tok_rows)
        real_part = jnp.einsum("aq,cqr->car", cos_block, shaped, precision=highest)
        imag_part = -jnp.einsum("aq,cqr->car", sin_block, shaped, precision=highest)
        real_part, imag_part = twist(real_part, imag_part, cos_twist, sin_twist, -1.0)
        return complex_apply("br,car->cab", cos_row, sin_row, real_part, imag_part, -1.0)

    signal_real, signal_imag = to_spectrum(signal)
    impulse_real, impulse_imag = to_spectrum(impulse)
    product_real = signal_real * impulse_real - signal_imag * impulse_imag
    product_imag = signal_real * impulse_imag + signal_imag * impulse_real
    back_real, back_imag = complex_apply(
        "br,cab->car", cos_row, sin_row, product_real, product_imag, 1.0
    )
    back_real, back_imag = twist(back_real, back_imag, cos_twist, sin_twist, 1.0)
    convolved = (
        jnp.einsum("aq,car->cqr", cos_block, back_real, precision=highest)
        - jnp.einsum("aq,car->cqr", sin_block, back_imag, precision=highest)
    ) / full_length
    convolved = convolved.reshape(group_width, seq_length)
    gated_rows = (arrived_streams[2].astype(jnp.float32) * convolved).astype(jnp.bfloat16)
    own_taps = lax.dynamic_slice_in_dim(short_filter, ctx_index * group_width, group_width, 0)
    shaped = gated_rows.reshape(group_width, seq_length // tap_count, tap_count)
    previous = jnp.concatenate(
        [jnp.zeros((group_width, 1, tap_count), jnp.bfloat16), shaped[:, :-1]], axis=1
    )
    block_pairs = jnp.concatenate([previous, shaped], axis=2)
    filtered = jnp.einsum(
        "ckj,cbj->bkc", toeplitz(own_taps), block_pairs, preferred_element_type=jnp.float32
    )
    filtered = filtered.reshape(seq_length, group_width).astype(jnp.bfloat16)
    return lax.all_to_all(filtered, "ctx", split_axis=0, concat_axis=1, tiled=True)


def remote(src, dst, send_sem, recv_sem, device):
    return pltpu.make_async_remote_copy(
        src_ref=src, dst_ref=dst, send_sem=send_sem, recv_sem=recv_sem,
        device_id=device, device_id_type=MESH,
    )


def block_kernel(
    tok_ref, proj_ref, rates_ref, residues_ref, filter_ref, out_ref,
    tokb, wbuf, sendb, recvb, ratesb, residuesb, filterb,
    signal, gate, gated, taps, mixed, outb,
    local_sem, par_sem, wl_sem, ws_sem, wr_sem,
    tzs, tzr, txs, txr, tcs, tcr, ps_sem, pr_sem, ol_sem, os_sem, or_sem,
):
    rows = tok_ref.shape[0]
    depth = proj_ref.shape[1]
    width = wbuf.shape[3]
    span = PAIR * depth
    ctx_count = lax.axis_size("ctx")
    zc = ctx_count // PAIR
    held = zc // 2
    seq = rows * ctx_count
    steps = seq // CHUNKS
    tile = sendb.shape[2] // pr_sem.shape[1]
    tiles = seq // tile
    modes = rates_ref.shape[0]
    tap_count = filter_ref.shape[1]
    ctx = lax.axis_index("ctx")
    ch = lax.axis_index("ch")
    mz, mx = ctx // PAIR, ctx % PAIR
    core = ch % 2
    mate = {"ch": ch + 1 - 2 * core}
    across = {"ctx": ctx + 1 - 2 * mx}
    half = rows // 2
    low = (mz < held).astype(jnp.int32)
    at_end = jnp.logical_or(mz == 0, mz == zc - 1)
    interior = jnp.logical_and(mz > 0, mz < zc - 1)

    def at_z(z):
        return {"ctx": z * PAIR + mx}

    def near(j):
        return low * (zc - 1 - j) + (1 - low) * j

    def far(j):
        return low * j + (1 - low) * (zc - 1 - j)

    def order(i):
        return near(i // 2) if i % 2 == 0 else far(i // 2)

    def cols(z):
        return pl.ds(pl.multiple_of(z * span, 128), span)

    def block(z, x):
        return pl.ds(pl.multiple_of((z * PAIR + x) * rows, 16), rows)

    def half_block(z, x):
        return pl.ds(pl.multiple_of((z * PAIR + x) * rows + core * half, 16), half)

    def group(d, x):
        return pl.ds(pl.multiple_of((d * PAIR + x) * width, 128), width)

    def tile_rows(t):
        return pl.ds(pl.multiple_of(t * tile, 16), tile)

    k_rows = pl.ds(pl.multiple_of(mx * depth, 16), depth)
    my_half = pl.ds(pl.multiple_of(core * half, 16), half)

    own_tok = pltpu.make_async_copy(tok_ref.at[:, cols(mz)], tokb.at[block(mz, mx)], local_sem)
    own_tok.start()
    own_w = []
    for i in range(zc):
        d = order(i)
        own_w.append(
            pltpu.make_async_copy(
                proj_ref.at[:, :, group(d, mx)], wbuf.at[d, :, k_rows], wl_sem.at[i]
            )
        )
        own_w[-1].start()
    own_par = []
    for j in range(held):
        place = group(far(j), mx)
        for n, (from_ref, to_ref) in enumerate((
            (rates_ref.at[:, place], ratesb.at[j]),
            (residues_ref.at[:, place], residuesb.at[j]),
            (filter_ref.at[place, :], filterb.at[j]),
        )):
            own_par.append(pltpu.make_async_copy(from_ref, to_ref, par_sem.at[3 * j + n]))
            own_par[-1].start()

    barrier = pltpu.get_barrier_semaphore()
    for o in range(1, ctx_count):
        pl.semaphore_signal(
            barrier, inc=1, device_id={"ctx": (ctx + o) % ctx_count}, device_id_type=MESH
        )
    pl.semaphore_signal(barrier, inc=1, device_id=mate, device_id_type=MESH)
    pl.semaphore_wait(barrier, ctx_count)

    z_copy, w_copy = {}, {}
    for o in range(1, zc):
        zt = (mz + o) % zc
        z_copy[o] = remote(
            tok_ref.at[my_half, cols(zt)], tokb.at[half_block(mz, mx)],
            tzs.at[o], tzr.at[o], at_z(zt),
        )
        z_copy[o].start()
    remote(
        tok_ref.at[my_half, cols(mz)], tokb.at[half_block(mz, mx)],
        txs.at[0], txr.at[0], across,
    ).start()

    def send_weights(i):
        d = order(i)
        w_copy[i] = remote(
            proj_ref.at[:, :, group(d, 1 - mx)], wbuf.at[d, :, k_rows],
            ws_sem.at[i], wr_sem.at[i], across,
        )
        w_copy[i].start()

    send_weights(0)

    def source(n):
        return low * n + (1 - low) * (zc - 1 - n)

    def z_forward(n):
        zs = source(n)
        o = (mz - zs + zc) % zc

        @pl.when(zs != mz)
        def _():
            here = tokb.at[half_block(zs, mx)]
            pltpu.make_async_copy(here, here, tzr.at[o]).wait()
            remote(here, here, txs.at[o], txr.at[o], across).start()
            remote(here, here, tcs.at[o], tcr.at[o], mate).start()

    def x_forward(n):
        zs = source(n)
        o = (mz - zs + zc) % zc
        here = tokb.at[half_block(zs, 1 - mx)]
        pltpu.make_async_copy(here, here, txr.at[o]).wait()
        remote(here, here, tcs.at[zc + o], tcr.at[zc + o], mate).start()

    def tokens_here(n):
        zs = source(n)
        o = (mz - zs + zc) % zc
        here = tokb.at[half_block(zs, mx)]

        @pl.when(zs != mz)
        def _():
            pltpu.make_async_copy(here, here, tcr.at[o]).wait()

        @pl.when(zs == mz)
        def _():
            own_tok.wait()

        pltpu.make_async_copy(here, here, tcr.at[zc + o]).wait()

    def hop(d, t):
        to = mz + 2 * (d >= held).astype(jnp.int32) - 1
        here = tile_rows(t)
        return remote(
            sendb.at[d, :, here, :], recvb.at[d, :, here, :],
            ps_sem.at[d, t], pr_sem.at[d, t], at_z(to),
        )

    def weights_here(i):
        own_w[i].wait()
        w_copy[i].wait_recv()

    def products(d, t):
        block_tok = tokb[tile_rows(t), :]
        return [
            jnp.dot(block_tok, wbuf[d, k], preferred_element_type=jnp.float32)
            for k in range(3)
        ]

    def arrived(d, t):
        here = tile_rows(t)
        pltpu.make_async_copy(
            sendb.at[d, :, here, :], recvb.at[d, :, here, :], pr_sem.at[d, t]
        ).wait()
        return [recvb[d, k, here, :].astype(jnp.float32) for k in range(3)]

    def pass_on(d, t):
        mine = products(d, t)
        before = arrived(d, t)
        for k in range(3):
            sendb[d, k, tile_rows(t), :] = (mine[k] + before[k]).astype(jnp.bfloat16)
        hop(d, t).start()

    def first_products(d, t):
        mine = products(d, t)
        for k in range(3):
            sendb[d, k, tile_rows(t), :] = mine[k].astype(jnp.bfloat16)
        hop(d, t).start()

    z_forward(0)
    for n in range(zc):
        if n + 1 < zc:
            z_forward(n + 1)
        x_forward(n)
        if n + 1 == zc - 1:
            for i in range(1, zc):
                send_weights(i)
        tokens_here(n)

        @pl.when(at_end)
        def _():
            if n == 0:
                weights_here(0)
            for part in range(PAIR * rows // tile):
                flow = n * (PAIR * rows // tile) + part
                first_products(near(0), low * flow + (1 - low) * (tiles - 1 - flow))

    @pl.when(interior)
    def _():
        for j in range(held):
            weights_here(2 * j)
            weights_here(2 * j + 1)

            @pl.loop(0, tiles)
            def _(t):
                pass_on(near(j), low * t + (1 - low) * (tiles - 1 - t))

                @pl.when(t > 0)
                def _():
                    pass_on(far(j), low * (tiles - t) + (1 - low) * (t - 1))

            pass_on(far(j), (1 - low) * (tiles - 1))

    wide = (CHUNKS, width)
    zero = jnp.zeros(wide, jnp.float32)
    peers = [(ctx + o) % ctx_count for o in range(1, ctx_count)]
    piece = rows // PIECES

    def leave(j, h, o):
        p = peers[o]
        here = pl.ds(pl.multiple_of(p * rows + h * piece, 16), piece)
        place = far(j) * PAIR + mx
        return remote(
            outb.at[j, here, :], out_ref.at[pl.ds(h * piece, piece), group(far(j), mx)],
            os_sem.at[j, h, o], or_sem.at[place, h], {"ctx": p},
        )

    def stay(j):
        here = pl.ds(pl.multiple_of(ctx * rows, 16), rows)
        return pltpu.make_async_copy(
            outb.at[j, here, :], out_ref.at[:, group(far(j), mx)], ol_sem.at[j]
        )

    def mix(j):
        rates = ratesb[j]
        weights = residuesb[j] * jnp.sqrt(2.0 * rates)
        taps[...] = filterb[j].astype(jnp.float32).T
        decay = jnp.exp(-rates)
        decays = [jnp.broadcast_to(decay[m : m + 1], wide) for m in range(modes)]
        gains = [jnp.broadcast_to(weights[m : m + 1], wide) for m in range(modes)]
        ids = lax.broadcasted_iota(jnp.int32, wide, 0)

        def row(ref, s):
            return ref[pl.ds(s, CHUNKS, stride=steps), :]

        def advance(s, states):
            x = row(signal, s)
            return tuple(decays[m] * states[m] + x for m in range(modes))

        ends = lax.fori_loop(0, steps, advance, (zero,) * modes, unroll=4)
        starts = []
        for m in range(modes):
            total = ends[m]
            shift = 1
            while shift < CHUNKS:
                factor = jnp.exp(-rates[m : m + 1] * float(steps * shift))
                total = total + jnp.where(ids >= shift, factor * pltpu.roll(total, shift, 0), 0.0)
                shift *= 2
            starts.append(jnp.where(ids >= 1, pltpu.roll(total, 1, 0), 0.0))

        def emit(s, states):
            states = advance(s, states)
            terms = [gains[m] * states[m] for m in range(modes)]
            while len(terms) > 1:
                terms = [a + b for a, b in zip(terms[::2], terms[1::2])] + terms[len(terms) & ~1 :]
            value = row(gate, s) * terms[0]
            gated[steps + s] = value
            gated[s] = jnp.where(ids >= 1, pltpu.roll(value, 1, 0), 0.0)
            return states

        lax.fori_loop(0, steps, emit, tuple(starts), unroll=2)

        out_block, tap_block = 16, 8
        for h in range(PIECES):
            @pl.loop(h * piece // out_block, (h + 1) * piece // out_block)
            def _(b):
                base = b * out_block

                def add_taps(kb, sums):
                    first = steps + base - kb * tap_block - (tap_block - 1)
                    window = [gated[first + i] for i in range(out_block + tap_block - 1)]
                    sums = list(sums)
                    for k in range(tap_block):
                        tap = jnp.broadcast_to(taps[pl.ds(kb * tap_block + k, 1), :], wide)
                        for i in range(out_block):
                            sums[i] = sums[i] + tap * window[i + tap_block - 1 - k]
                    return tuple(sums)

                sums = lax.fori_loop(0, tap_count // tap_block, add_taps, (zero,) * out_block)
                for i in range(out_block):
                    mixed[pl.ds(base + i, CHUNKS, stride=steps), :] = sums[i]

            for c in range(CHUNKS):
                here = pl.ds(c * rows + h * piece, piece)
                outb[j, here, :] = mixed[here, :].astype(outb.dtype)
            for o in range(ctx_count - 1):
                leave(j, h, o).start()
        stay(j).start()

    @pl.when(at_end)
    def _():
        for j in range(1, held):
            weights_here(2 * j)

            @pl.loop(0, tiles)
            def _(t):
                first_products(near(j), low * t + (1 - low) * (tiles - 1 - t))

        for j in range(held):
            weights_here(2 * j + 1)
            for n in range(3):
                own_par[3 * j + n].wait()

            @pl.loop(0, tiles)
            def _(n):
                t = low * (tiles - 1 - n) + (1 - low) * n
                mine = products(far(j), t)
                before = arrived(far(j), t)
                sums = [mine[k] + before[k] for k in range(3)]
                signal[tile_rows(t), :] = sums[0] * sums[1]
                gate[tile_rows(t), :] = sums[2]

            mix(j)

        for j in range(held):
            stay(j).wait()

            @pl.loop(0, tiles)
            def _(t):
                hop(near(j), t).wait_send()

            for h in range(PIECES):
                for o in range(ctx_count - 1):
                    leave(j, h, o).wait_send()

    @pl.when(interior)
    def _():
        for par in own_par:
            par.wait()
        for j in range(held):
            @pl.loop(0, tiles)
            def _(t):
                hop(near(j), t).wait_send()
                hop(far(j), t).wait_send()

    for group_of in (z_copy, w_copy):
        for key in group_of:
            group_of[key].wait_send()
    sent = tokb.at[half_block(mz, mx)]
    for o in range(zc):
        remote(sent, sent, txs.at[o], txr.at[o], across).wait_send()
        remote(sent, sent, tcs.at[zc + o], tcr.at[zc + o], mate).wait_send()
        if o > 0:
            remote(sent, sent, tcs.at[o], tcr.at[o], mate).wait_send()
    for d in range(zc):
        owner_row = 0 if d < held else zc - 1
        for x in range(PAIR):
            @pl.when(ctx != owner_row * PAIR + x)
            def _():
                for h in range(PIECES):
                    landed = out_ref.at[
                        pl.ds(h * piece, piece), pl.ds((d * PAIR + x) * width, width)
                    ]
                    pltpu.make_async_copy(
                        outb.at[0, pl.ds(0, piece), :], landed, or_sem.at[d * PAIR + x, h]
                    ).wait()


def per_device_kernels(tokens, projections, decay_rates, residues, short_filter):
    rows = tokens.shape[0]
    depth, channels = projections.shape[1:]
    ctx_count = lax.axis_size("ctx")
    zc = ctx_count // PAIR
    held = zc // 2
    width = channels // ctx_count
    seq = rows * ctx_count
    steps = seq // CHUNKS
    tiles = seq // TILE
    modes = decay_rates.shape[1]
    tap_count = short_filter.shape[1]
    dma = pltpu.SemaphoreType.DMA
    f32, bf16 = jnp.float32, jnp.bfloat16
    return pl.pallas_call(
        block_kernel,
        out_shape=jax.ShapeDtypeStruct((rows, channels), bf16),
        in_specs=[pl.BlockSpec(memory_space=pltpu.HBM)] * 5,
        out_specs=pl.BlockSpec(memory_space=pltpu.VMEM),
        scratch_shapes=[
            pltpu.VMEM((seq, PAIR * depth), bf16),
            pltpu.VMEM((zc, 3, PAIR * depth, width), bf16),
            pltpu.VMEM((zc, 3, seq, width), bf16),
            pltpu.VMEM((zc, 3, seq, width), bf16),
            pltpu.VMEM((held, modes, width), f32),
            pltpu.VMEM((held, modes, width), f32),
            pltpu.VMEM((held, width, tap_count), bf16),
            pltpu.VMEM((seq, width), f32),
            pltpu.VMEM((seq, width), f32),
            pltpu.VMEM((2 * steps, CHUNKS, width), f32),
            pltpu.VMEM((tap_count, width), f32),
            pltpu.VMEM((seq, width), f32),
            pltpu.VMEM((held, seq, width), bf16),
            dma, dma((3 * held,)), dma((zc,)), dma((zc,)), dma((zc,)),
            dma((zc,)), dma((zc,)), dma((zc,)), dma((zc,)),
            dma((2 * zc,)), dma((2 * zc,)), dma((zc, tiles)), dma((zc, tiles)),
            dma((held,)), dma((held, PIECES, ctx_count - 1)), dma((ctx_count, PIECES)),
        ],
        compiler_params=pltpu.CompilerParams(
            collective_id=0, has_side_effects=True, vmem_limit_bytes=48 * 1024 * 1024
        ),
        name="block",
    )(tokens, projections, decay_rates.T, residues.T, short_filter)


def kernels_fit(tokens, projections, short_filter):
    ctx_count = lax.axis_size("ctx")
    rows = tokens.shape[0]
    depth, channels = projections.shape[1:]
    tap_count = short_filter.shape[1]
    return (
        ctx_count == CHUNKS and lax.axis_size("ch") % 2 == 0
        and channels == ctx_count * LANES and rows % (16 * PIECES) == 0 and depth % 128 == 0
        and PAIR * rows % TILE == 0 and tap_count % 8 == 0 and tap_count <= rows
        and rows * ctx_count <= 2048
    )


def per_device(tokens, projections, decay_rates, residues, short_filter):
    plan = per_device_kernels if kernels_fit(tokens, projections, short_filter) else per_device_general
    return plan(tokens, projections, decay_rates, residues, short_filter)


def solution(mesh):
    in_specs = (P("ctx", None), P(None, "ctx", "ch"), P("ch", None), P("ch", None), P("ch", None))
    out_specs = P("ctx", "ch")
    return jax.shard_map(
        per_device, mesh=mesh, in_specs=in_specs, out_specs=out_specs, check_vma=False
    )
```
